32 devices in a mesh: pipe: 2 (over y), row: 4 (over z), col: 4 (over x, core).
Axes of the slice: x: 2, y: 2, z: 4, core: 2. Of those that a mesh axis runs over, the one named last changes fastest.
Arguments:
- tokens: bfloat16 [2, 128, 4096], P('pipe', 'row', 'col'), may hold values from -12 to 12
- norm_gain: float32 [2, 4096], P('pipe', 'col'), may hold values from 0.5 to 2
- gate_weight: bfloat16 [2, 4096, 14336], P('pipe', 'col', 'row'), may hold values from -0.09375 to 0.09375
- up_weight: bfloat16 [2, 4096, 14336], P('pipe', 'col', 'row'), may hold values from -0.09375 to 0.09375
- down_weight: bfloat16 [2, 14336, 4096], P('pipe', ('row', 'col')), may hold values from -0.046875 to 0.046875
Outputs:
- handed: bfloat16 [2, 128, 4096], P('pipe', 'row', 'col')
The draws below stay inside these ranges and needn't reach their ends.
All inputs are finite; a program needn't handle non-finite values.
Results may differ from the reference program's by a relative error of at most 0.024.
Values may be sent and summed in bfloat16 or wider, within the bound.
No kernel may reach another device: no remote copies, remote signals or barrier semaphores. Data moves between devices by JAX's collectives and lax.ppermute only.
A program may use at most 64 MiB of HBM per device.

```python
import math
import jax
import jax.numpy as jnp
from jax import lax

D = 4096
FF = 14336
TOKENS = 128
SECTIONS = 2
N_ROW = 4
N_COL = 4


def draw_tokens(key, part):
    key_base, key_jitter, key_rows = jax.random.split(key, 3)
    column = jnp.arange(D, dtype=jnp.float32)
    rising = jnp.sqrt(1.0 + 2.0 * column / max(D - 1, 1))
    jitter = jnp.exp(jax.random.uniform(key_jitter, (SECTIONS, 1, D), jnp.float32, -0.5, 0.5))
    row_scale = jnp.exp(jax.random.uniform(key_rows, (SECTIONS, TOKENS, 1), jnp.float32, math.log(0.1), 0.0))
    base = jnp.clip(jax.random.normal(key_base, (SECTIONS, TOKENS, D), jnp.float32), -4.0, 4.0)
    return (base * rising * jitter * row_scale).astype(jnp.bfloat16)


def steps_of(stream_key, dims, cuts, low, top_value):
    def one(dim, blocks):
        heights = jax.random.uniform(jax.random.fold_in(jax.random.fold_in(stream_key, 6), dim), (blocks,), jnp.float32, low / len(cuts), top_value / len(cuts))
        return jnp.repeat(jnp.exp(heights), dims[dim] // blocks).reshape((-1,) + (1,) * (len(dims) - dim - 1))

    level = one(*cuts[0])
    for cut in cuts[1:]:
        level = level * one(*cut)
    return level


def gaussian(own_key, extent, width, limit, cuts=(), kind=jnp.bfloat16):
    array = width * jax.random.normal(own_key, extent, jnp.float32)
    if cuts:
        array = array * steps_of(own_key, extent, cuts, -0.22, 0.18)
    return jnp.clip(array, -limit, limit).astype(kind)


def setup_inputs(seed: int = 0) -> dict:
    keys = jax.random.split(jax.random.key(seed), 6)
    return {
        "tokens": draw_tokens(jax.random.fold_in(keys[5], 71), 0),
        "norm_gain": jnp.clip(jnp.exp(math.log(2.0) - 1.3862944 * jax.random.uniform(keys[1], (SECTIONS, D), jnp.float32) ** steps_of(keys[1], (SECTIONS, D), ((0, 2), (1, 4)), -0.2, 0.2)), 0.5, 2.0),
        "gate_weight": gaussian(keys[2], (SECTIONS, D, FF), D ** -0.5, 0.09375, ((0, 2), (1, 4), (2, 4))),
        "up_weight": gaussian(keys[3], (SECTIONS, D, FF), D ** -0.5, 0.09375, ((0, 2), (1, 4), (2, 4))),
        "down_weight": gaussian(keys[4], (SECTIONS, FF, D), FF ** -0.5, 0.046875, ((0, 2), (1, 16))),
    }


EPS = 1e-05

def reference(tokens, norm_gain, gate_weight, up_weight, down_weight):
    pieces = N_ROW * N_COL
    block_width = FF // pieces

    def one_section(section_args):
        inputs, gain, gate_w, up_w, down_w = section_args
        widened = inputs.astype(jnp.float32)
        mean_square = lax.optimization_barrier(jnp.mean(widened * widened, axis=1, keepdims=True))
        normed = (widened * lax.rsqrt(mean_square + EPS) * gain.astype(jnp.float32)[None, :]).astype(jnp.bfloat16)
        gate_value = jnp.dot(normed, gate_w, preferred_element_type=jnp.float32)
        up_value = jnp.dot(normed, up_w, preferred_element_type=jnp.float32)
        hidden = (jax.nn.silu(gate_value) * up_value).astype(jnp.bfloat16)
        hidden_blocks = hidden.reshape(TOKENS, pieces, block_width).transpose(1, 0, 2)
        down_blocks = down_w.reshape(pieces, block_width, D)

        def add_block(total, pair):
            hidden_part, weight_part = pair
            rounded = jnp.dot(hidden_part, weight_part, preferred_element_type=jnp.float32).astype(jnp.bfloat16)
            rounded = lax.optimization_barrier(rounded)
            return (total + rounded.astype(jnp.float32), None)
        total, _ = lax.scan(add_block, jnp.zeros((TOKENS, D), jnp.float32), (hidden_blocks, down_blocks))
        branch_out = total.astype(jnp.bfloat16)
        return (widened + branch_out.astype(jnp.float32)).astype(jnp.bfloat16)
    layer_out = lax.map(one_section, (tokens, norm_gain, gate_weight, up_weight, down_weight))
    return jnp.roll(layer_out, 1, axis=0)
```

```python
import functools

import jax
import jax.numpy as jnp
from jax import lax
from jax.experimental import pallas as pl
from jax.experimental.pallas import tpu as pltpu
from jax.sharding import PartitionSpec as P

EPS = 1e-05
LANES = 128
F32 = jnp.float32
BF16 = jnp.bfloat16


def flipped(index, mask):
    bit = 1
    while bit <= mask:
        if mask & bit:
            index = index + bit - 2 * bit * ((index // bit) % 2)
        bit *= 2
    return index


def swapped(value, axis, mask):
    count = lax.axis_size(axis)
    return lax.ppermute(value, axis, [(i, i ^ mask) for i in range(count)])


def masks_of(count):
    return [1 << b for b in range(count.bit_length() - 1)]


placed_in = pltpu.with_memory_space_constraint


def call(body, name, operands, outs, scratch=(), cost=None):
    return pl.pallas_call(
        body,
        name=name,
        in_specs=[
            pl.BlockSpec(memory_space=pltpu.VMEM if held else pltpu.HBM) for _, held in operands
        ],
        out_shape=[pltpu.VMEM(shape, dtype) for shape, dtype in outs],
        out_specs=[pl.BlockSpec(memory_space=pltpu.VMEM) for _ in outs],
        scratch_shapes=list(scratch),
        cost_estimate=cost,
        compiler_params=pltpu.CompilerParams(vmem_limit_bytes=16 * 1024 * 1024),
    )(*[placed_in(a, pltpu.VMEM if held else pltpu.HBM) for a, held in operands])


def dot(a, b):
    return jnp.dot(a, b, preferred_element_type=F32)


def load_columns(gate_ref, up_ref, gate_out, up_out, sems):
    count, _, width = gate_out.shape
    mine = lax.axis_index("col")
    copies = []
    for k in reversed(range(count)):
        columns = pl.ds(pl.multiple_of(flipped(mine, k) * width, LANES), width)
        for i, (ref, out) in enumerate(((gate_ref, gate_out), (up_ref, up_out))):
            copies.append(pltpu.make_async_copy(ref.at[0, :, columns], out.at[k], sems.at[k, i]))
    for copy in copies:
        copy.start()
    for copy in copies:
        copy.wait()


def scale_and_first(k, slots, *refs):
    tokens, (gain_ref, gate_ref, up_ref, x_out, s_out, p_out) = refs[:slots], refs[slots:]
    rows = tokens[0].shape[0]
    sums = []
    for i, ref in enumerate(tokens):
        wide = ref[...].astype(F32)
        x_out[pl.ds(i * rows, rows), :] = (wide * gain_ref[...]).astype(BF16)
        sums.append(jnp.sum(wide * wide, axis=1, keepdims=True))
    p_out[0] = dot(x_out[...], gate_ref[k]).astype(p_out.dtype)
    p_out[1] = dot(x_out[...], up_ref[k]).astype(p_out.dtype)
    if slots * rows < LANES:
        sums.append(jnp.zeros((LANES - slots * rows, 1), F32))
    column = jnp.concatenate(sums, axis=0)
    s_out[...] = jnp.transpose(jnp.broadcast_to(column, (LANES, LANES)))[:1]


def product(k, x_ref, gate_ref, up_ref, p_out):
    p_out[0] = dot(x_ref[...], gate_ref[k]).astype(p_out.dtype)
    p_out[1] = dot(x_ref[...], up_ref[k]).astype(p_out.dtype)


def product_and_load(x_ref, gate_ref, up_ref, down_ref, p_out, down_out, sems):
    count, _, width = down_out.shape
    mine = lax.axis_index("col")
    copies = []
    for k in reversed(range(count)):
        columns = pl.ds(pl.multiple_of(flipped(mine, k) * width, LANES), width)
        copies.append(pltpu.make_async_copy(down_ref.at[0, :, columns], down_out.at[k], sems.at[k]))
    for copy in copies:
        copy.start()
    product(0, x_ref, gate_ref, up_ref, p_out)
    for copy in copies:
        copy.wait()


def activate(scale, own_ref, near_ref, far_ref, s_refs, h_out):
    total = sum(s[...] for s in s_refs)
    column = jnp.transpose(jnp.broadcast_to(total, (LANES, LANES)))[: h_out.shape[0], :1]
    inverse = lax.rsqrt(column * scale + EPS)
    gate, up = (
        (own_ref[i] + near_ref[i].astype(F32) + far_ref[i].astype(F32)) * inverse for i in (0, 1)
    )
    h_out[...] = (gate / (1.0 + jnp.exp(-gate)) * up).astype(BF16)


def activate_and_down(scale, blocks, own_ref, near_ref, far_ref, sa, sb, down_ref, h_out, d_out):
    activate(scale, own_ref, near_ref, far_ref, (sa, sb), h_out)
    for i, k in enumerate(blocks):
        d_out[i] = dot(h_out[...], down_ref[k]).astype(BF16)


def down(blocks, h_ref, down_ref, d_out):
    for i, k in enumerate(blocks):
        d_out[i] = dot(h_ref[...], down_ref[k]).astype(BF16)


def added(*values):
    return sum(v.astype(F32) for v in values).astype(BF16)


def fast(tokens, norm_gain, gate_weight, up_weight, down_weight):
    rows, cols, pipes = lax.axis_size("row"), lax.axis_size("col"), lax.axis_size("pipe")
    _, count, depth = tokens.shape
    width = gate_weight.shape[2] // cols
    own = tokens[0]
    forward = [(p, (p + 1) % pipes) for p in range(pipes)]
    handed_tokens = lax.ppermute(own, "pipe", forward)
    slots = [own] + [swapped(own, "row", k) for k in range(1, rows)]
    gates, ups = call(
        load_columns,
        "load_columns",
        [(gate_weight, False), (up_weight, False)],
        [((cols, depth, width), BF16)] * 2,
        [pltpu.SemaphoreType.DMA((cols, 2))],
        pl.CostEstimate(flops=0, transcendentals=0, bytes_accessed=2 * gate_weight.size * 2 * 2),
    )
    m = rows * count
    weights = [(gates, True), (ups, True)]
    x, s, p3 = call(
        functools.partial(scale_and_first, 3, rows),
        "scale_and_first",
        [(slot, True) for slot in slots] + [(norm_gain, True)] + weights,
        [((m, depth), BF16), ((1, LANES), F32), ((2, m, width), BF16)],
    )
    r3 = swapped(p3, "col", 1)
    (p2,) = call(
        functools.partial(product, 2), "product2", [(x, True)] + weights, [((2, m, width), BF16)]
    )
    q2 = added(p2, r3)
    f2 = swapped(q2, "col", 2)
    (p1,) = call(
        functools.partial(product, 1), "product1", [(x, True)] + weights, [((2, m, width), BF16)]
    )
    r1 = swapped(p1, "col", 1)
    p0, downs = call(
        product_and_load,
        "product_and_load",
        [(x, True)] + weights + [(down_weight, False)],
        [((2, m, width), F32), ((cols, width, depth), BF16)],
        [pltpu.SemaphoreType.DMA((cols,))],
    )
    s1 = s + swapped(s, "col", 1)
    s2 = swapped(s1, "col", 2)
    h, e1 = call(
        functools.partial(activate_and_down, 1.0 / (depth * cols), (1, 3)),
        "activate_and_down",
        [(p0, True), (r1, True), (f2, True), (s1, True), (s2, True), (downs, True)],
        [((m, width), BF16), ((2, m, depth), BF16)],
    )
    t1 = swapped(e1, "col", 1)
    (e0,) = call(
        functools.partial(down, (0, 2)), "down", [(h, True), (downs, True)], [((2, m, depth), BF16)]
    )
    u2 = added(e0[1], t1[1])
    v2 = swapped(u2, "col", 2)
    total = added(e0[0], t1[0], v2)
    parts = []
    for k in range(rows):
        pairs = [
            (p * rows + r, forward[p][1] * rows + (r ^ k)) for p in range(pipes) for r in range(rows)
        ]
        parts.append(lax.ppermute(total[k * count : (k + 1) * count], ("pipe", "row"), pairs))
    branch_out = added(*parts)
    return added(handed_tokens, branch_out)[None]


def plain(tokens, norm_gain, gate_weight, up_weight, down_weight):
    rows, cols, pipes = lax.axis_size("row"), lax.axis_size("col"), lax.axis_size("pipe")
    _, count, depth = tokens.shape
    wide = tokens[0].astype(F32)
    squares = lax.psum(jnp.sum(wide * wide, axis=1), "col")
    inverse = lax.rsqrt(squares / (depth * cols) + EPS)
    normed = (wide * inverse[:, None] * norm_gain).astype(BF16)
    piece = lax.all_gather(normed, "row", axis=0, tiled=True)
    sums = jnp.stack([dot(piece, gate_weight[0]), dot(piece, up_weight[0])])
    summed = lax.psum_scatter(sums.astype(BF16), "col", scatter_dimension=2, tiled=True).astype(F32)
    hidden = (jax.nn.silu(summed[0]) * summed[1]).astype(BF16)
    terms = dot(hidden, down_weight[0]).reshape(rows, count, cols, depth).transpose(0, 2, 1, 3)
    terms = terms.reshape(rows * cols, count, depth).astype(BF16)
    branch_out = lax.psum_scatter(terms, ("row", "col"), scatter_dimension=0, tiled=True)[0]
    layer_out = added(tokens[0], branch_out)
    return lax.ppermute(layer_out, "pipe", [(p, (p + 1) % pipes) for p in range(pipes)])[None]


def local(tokens, norm_gain, gate_weight, up_weight, down_weight):
    rows, cols = lax.axis_size("row"), lax.axis_size("col")
    _, count, depth = tokens.shape
    width = gate_weight.shape[2] // cols
    fits = (
        cols == 4
        and rows & (rows - 1) == 0
        and rows * count <= LANES
        and count % 16 == 0
        and depth % LANES == 0
        and width % LANES == 0
    )
    form = fast if fits else plain
    return form(tokens, norm_gain, gate_weight, up_weight, down_weight)


def solution(mesh):
    placed = (
        P("pipe", "row", "col"),
        P("pipe", "col"),
        P("pipe", "col", "row"),
        P("pipe", "col", "row"),
        P("pipe", ("row", "col"), None),
    )
    return jax.shard_map(
        local, mesh=mesh, in_specs=placed, out_specs=P("pipe", "row", "col"), check_vma=False
    )
```

```python
import functools

import jax
import jax.numpy as jnp
from jax import lax
from jax.experimental import pallas as pl
from jax.experimental.pallas import tpu as pltpu
from jax.sharding import PartitionSpec as P

EPS = 1e-05
LANES = 128
F32 = jnp.float32
BF16 = jnp.bfloat16


def flipped(index, mask):
    bit = 1
    while bit <= mask:
        if mask & bit:
            index = index + bit - 2 * bit * ((index // bit) % 2)
        bit *= 2
    return index


def swapped(value, axis, mask):
    count = lax.axis_size(axis)
    return lax.ppermute(value, axis, [(i, i ^ mask) for i in range(count)])


def masks_of(count):
    return [1 << b for b in range(count.bit_length() - 1)]


placed_in = pltpu.with_memory_space_constraint


COST = {'load': 62262000000, 'first': 8762800000, 'product2': 0, 'product1': 0, 'product0': 42661000000, 'joined': 2075399999, 'activate_far': 9915800000, 'down_far': 8878100000, 'activate_near': 0, 'down_near': 0}


def call(body, name, outs, held, streamed=(), after=(), copies=0, cost=0):
    fixed = len(held) + len(streamed)

    def run(*refs):
        body(*refs[:fixed], *refs[fixed + len(after) :])

    spaces = [pltpu.VMEM] * len(held) + [pltpu.HBM] * len(streamed)
    return pl.pallas_call(
        run,
        name=name,
        in_specs=[pl.BlockSpec(memory_space=s) for s in spaces]
        + [pl.BlockSpec(memory_space=pl.ANY)] * len(after),
        out_shape=[pltpu.VMEM(shape, dtype) for shape, dtype in outs],
        out_specs=[pl.BlockSpec(memory_space=pltpu.VMEM)] * len(outs),
        scratch_shapes=[pltpu.SemaphoreType.DMA((copies,))] if copies else [],
        cost_estimate=pl.CostEstimate(flops=COST[name], transcendentals=0, bytes_accessed=0),
        compiler_params=pltpu.CompilerParams(vmem_limit_bytes=16 * 1024 * 1024),
    )(*[placed_in(a, s) for a, s in zip([*held, *streamed], spaces)], *after)


def dot(a, b):
    return jnp.dot(a, b, preferred_element_type=F32)


def copies_of(pairs, sems):
    copies = []
    for k in reversed(range(pairs[0][1].shape[0])):
        for source, held in pairs:
            width = held.shape[2]
            columns = pl.ds(pl.multiple_of(flipped(lax.axis_index("col"), k) * width, LANES), width)
            copy = pltpu.make_async_copy(
                source.at[0, :, columns], held.at[k], sems.at[len(copies)]
            )
            copy.start()
            copies.append(copy)
    return copies


def load(gate_ref, up_ref, gate_out, up_out, sems):
    for copy in copies_of([(gate_ref, gate_out), (up_ref, up_out)], sems):
        copy.wait()


def in_terms(column):
    lane = lax.broadcasted_iota(jnp.int32, (column.shape[0], LANES), 1)
    terms = jnp.zeros(lane.shape, F32)
    for i in range(3):
        part = column.astype(BF16).astype(F32)
        terms = jnp.where(lane == i, part, terms)
        column = column - part
    return terms.astype(BF16)


def from_terms(tile):
    return jnp.sum(tile.astype(F32), axis=1, keepdims=True)


def products(k, x_ref, gate_ref, up_ref, outs):
    width = gate_ref.shape[2]
    for i, ref in enumerate((gate_ref, up_ref)):
        both = dot(x_ref[...], ref[k])
        row = 0
        for out in outs:
            here = slice(row, row + out.shape[0])
            out[:, i * width : (i + 1) * width] = both[here].astype(out.dtype)
            row += out.shape[0]


def scale_and_first(k, *refs):
    *tokens, gain_ref, gate_ref, up_ref, x_out, s_out, a_out, b_out = refs
    rows = tokens[0].shape[0]
    for i, ref in enumerate(tokens):
        wide = ref[...].astype(F32)
        here = slice(i * rows, (i + 1) * rows)
        x_out[here, :] = (wide * gain_ref[...]).astype(BF16)
        s_out[here, :] = in_terms(jnp.sum(wide * wide, axis=1, keepdims=True))
    products(k, x_out, gate_ref, up_ref, (a_out, b_out))
    m, start = a_out.shape[0], a_out.shape[1] - LANES
    a_out[:, start:] = s_out[:m, :]
    b_out[:, start:] = s_out[m:, :]


def product(k, x_ref, gate_ref, up_ref, out):
    products(k, x_ref, gate_ref, up_ref, (out,))


def product_and_load(k, x_ref, gate_ref, up_ref, down_ref, out, down_out, sems):
    copies = copies_of([(down_ref, down_out)], sems)
    products(k, x_ref, gate_ref, up_ref, (out,))
    for copy in copies:
        copy.wait()


def joined(first, p_ref, s_ref, r_ref, out):
    count, width = out.shape[0], p_ref.shape[1]
    here = slice(first, first + count)
    out[:, :width] = (p_ref[here, :].astype(F32) + r_ref[:, :width].astype(F32)).astype(BF16)
    out[:, width:] = in_terms(from_terms(s_ref[here, :]) + from_terms(r_ref[:, width:]))


def joined_and_own(first, p_ref, s_ref, r_ref, own_ref, out, own_out):
    own_out[...] = own_ref[...]
    joined(first, p_ref, s_ref, r_ref, out)


def activate_and_down(first, factor, blocks, p_ref, near_ref, s_ref, far_ref, sib_ref, down_ref, h_out, d_out):
    count, width = h_out.shape
    here = slice(first, first + count)
    tail = slice(2 * width, 2 * width + LANES)
    tiles = (s_ref[here, :], sib_ref[:, tail], far_ref[:, tail])
    inverse = lax.rsqrt(sum(from_terms(tile) for tile in tiles) * factor + EPS)
    gate, up = (
        (p_ref[here, at] + near_ref[here, at].astype(F32) + far_ref[:, at].astype(F32)) * inverse
        for at in (slice(0, width), slice(width, 2 * width))
    )
    h_out[...] = (gate / (1.0 + jnp.exp(-gate)) * up).astype(BF16)
    down(blocks, h_out, down_ref, d_out)


def down(blocks, h_ref, down_ref, d_out):
    for i, k in enumerate(blocks):
        d_out[i] = dot(h_ref[...], down_ref[k]).astype(BF16)


def added(*values):
    return sum(v.astype(F32) for v in values).astype(BF16)


def fast(tokens, norm_gain, gate_weight, up_weight, down_weight):
    rows, cols, pipes = (lax.axis_size(a) for a in ("row", "col", "pipe"))
    _, count, depth = tokens.shape
    width = gate_weight.shape[2] // cols
    part = functools.partial
    own = tokens[0]
    m = rows // 2 * count
    forward = [(p, (p + 1) % pipes) for p in range(pipes)]
    slots = [own] + [swapped(own, "row", k) for k in range(1, rows)]
    order = [2, 3, 0, 1]
    weights = call(
        load, "load", [((cols, depth, width), BF16)] * 2, [], [gate_weight, up_weight],
        copies=2 * cols, cost=4 * gate_weight.size * 2,
    )
    payload, sums = ((m, 2 * width + LANES), BF16), ((2 * m, 2 * width), BF16)
    x, s, p3f, p3n = call(
        part(scale_and_first, 3), "first",
        [((2 * m, depth), BF16), ((2 * m, LANES), BF16), payload, payload],
        [slots[k] for k in order] + [norm_gain, *weights],
    )
    r3f = swapped(p3f, "col", 1)
    r3n = swapped(p3n, "col", 1)
    (p2,) = call(part(product, 2), "product2", [sums], [x, *weights])
    (q2f,) = call(part(joined, 0), "joined", [payload], [p2, s, r3f])
    f2f = swapped(q2f, "col", 2)
    q2n, own_copy = call(
        part(joined_and_own, m), "joined", [payload, (own.shape, BF16)], [p2, s, r3n, own], (), [q2f]
    )
    f2n = swapped(q2n, "col", 2)
    handed_tokens = lax.ppermute(own_copy, "pipe", forward)
    (p1,) = call(part(product, 1), "product1", [sums], [x, *weights])
    r1 = swapped(p1, "col", 1)
    p0, downs = call(
        part(product_and_load, 0), "product0",
        [((2 * m, 2 * width), F32), ((cols, width, depth), BF16)],
        [x, *weights], [down_weight], [q2n], cols,
    )

    def hidden_and_down(first, f2, r3, after, which):
        h, e1 = call(
            part(activate_and_down, first, 1.0 / (depth * cols), (1, 3)), "activate_" + which,
            [((m, width), BF16), ((2, m, depth), BF16)], [p0, r1, s, f2, r3, downs], (), after,
        )
        t1 = swapped(e1, "col", 1)
        (e0,) = call(part(down, (0, 2)), "down_" + which, [((2, m, depth), BF16)], [h, downs])
        return added(e0, t1)

    w = hidden_and_down(0, f2f, r3f, [handed_tokens], "far")
    u = hidden_and_down(m, f2n, r3n, [w], "near")
    w = added(w[0], swapped(w[1], "col", 2))
    w = added(w[:count], swapped(w[count:], "row", 1))
    n = added(u[0], swapped(u[1], "col", 2))

    def onward(value, k):
        pairs = [(p * rows + r, q * rows + (r ^ k)) for p, q in forward for r in range(rows)]
        return lax.ppermute(value, ("pipe", "row"), pairs)

    parts = [onward(n[:count], 0), onward(n[count:], 1), onward(w, 2)]
    return added(handed_tokens, added(*parts))[None]


def plain(tokens, norm_gain, gate_weight, up_weight, down_weight):
    rows, cols, pipes = lax.axis_size("row"), lax.axis_size("col"), lax.axis_size("pipe")
    _, count, depth = tokens.shape
    wide = tokens[0].astype(F32)
    squares = lax.psum(jnp.sum(wide * wide, axis=1), "col")
    inverse = lax.rsqrt(squares / (depth * cols) + EPS)
    normed = (wide * inverse[:, None] * norm_gain).astype(BF16)
    piece = lax.all_gather(normed, "row", axis=0, tiled=True)
    sums = jnp.stack([dot(piece, gate_weight[0]), dot(piece, up_weight[0])])
    summed = lax.psum_scatter(sums.astype(BF16), "col", scatter_dimension=2, tiled=True).astype(F32)
    hidden = (jax.nn.silu(summed[0]) * summed[1]).astype(BF16)
    terms = dot(hidden, down_weight[0]).reshape(rows, count, cols, depth).transpose(0, 2, 1, 3)
    terms = terms.reshape(rows * cols, count, depth).astype(BF16)
    branch_out = lax.psum_scatter(terms, ("row", "col"), scatter_dimension=0, tiled=True)[0]
    layer_out = added(tokens[0], branch_out)
    return lax.ppermute(layer_out, "pipe", [(p, (p + 1) % pipes) for p in range(pipes)])[None]


def local(tokens, norm_gain, gate_weight, up_weight, down_weight):
    rows, cols = lax.axis_size("row"), lax.axis_size("col")
    _, count, depth = tokens.shape
    width = gate_weight.shape[2] // cols
    fits = (
        cols == 4
        and rows == 4
        and count % 16 == 0
        and depth % LANES == 0
        and width % LANES == 0
    )
    form = fast if fits else plain
    return form(tokens, norm_gain, gate_weight, up_weight, down_weight)


def solution(mesh):
    placed = (
        P("pipe", "row", "col"),
        P("pipe", "col"),
        P("pipe", "col", "row"),
        P("pipe", "col", "row"),
        P("pipe", ("row", "col"), None),
    )
    return jax.shard_map(
        local, mesh=mesh, in_specs=placed, out_specs=P("pipe", "row", "col"), check_vma=False
    )
```

```python
import functools

import jax
import jax.numpy as jnp
from jax import lax
from jax.experimental import pallas as pl
from jax.experimental.pallas import tpu as pltpu
from jax.sharding import PartitionSpec as P

EPS = 1e-05
LANES = 128
F32 = jnp.float32
BF16 = jnp.bfloat16


def flipped(index, mask):
    bit = 1
    while bit <= mask:
        if mask & bit:
            index = index + bit - 2 * bit * ((index // bit) % 2)
        bit *= 2
    return index


def swapped(value, axis, mask):
    count = lax.axis_size(axis)
    return lax.ppermute(value, axis, [(i, i ^ mask) for i in range(count)])


def masks_of(count):
    return [1 << b for b in range(count.bit_length() - 1)]


placed_in = pltpu.with_memory_space_constraint

COST = dict(
    pause=1000, first_near=100, next_near=100, first_far=100, next_far=100, joined_near=100, joined_far=100, product1=15, product0=1, activate_near=100, down_near=100, activate_far=100, down_far=1
)


def call(body, name, outs, held, streamed=(), after=(), copies=0):
    fixed = len(held) + len(streamed)

    def run(*refs):
        body(*refs[:fixed], *refs[fixed + len(after) :])

    spaces = [pltpu.VMEM] * len(held) + [pltpu.HBM] * len(streamed)
    return pl.pallas_call(
        run,
        name=name,
        in_specs=[pl.BlockSpec(memory_space=s) for s in spaces]
        + [pl.BlockSpec(memory_space=pl.ANY)] * len(after),
        out_shape=[pltpu.VMEM(shape, dtype) for shape, dtype in outs],
        out_specs=[pl.BlockSpec(memory_space=pltpu.VMEM)] * len(outs),
        scratch_shapes=[pltpu.SemaphoreType.DMA((copies,))] if copies else [],
        cost_estimate=pl.CostEstimate(
            flops=COST.get(name, 0) * 10**8, transcendentals=0, bytes_accessed=0
        ),
        compiler_params=pltpu.CompilerParams(vmem_limit_bytes=16 * 1024 * 1024),
    )(*[placed_in(a, s) for a, s in zip([*held, *streamed], spaces)], *after)


def dot(a, b):
    return jnp.dot(a, b, preferred_element_type=F32)


def block(k, width):
    return pl.ds(pl.multiple_of(flipped(lax.axis_index("col"), k) * width, LANES), width)


def in_terms(column):
    lane = lax.broadcasted_iota(jnp.int32, (column.shape[0], LANES), 1)
    terms = jnp.zeros(lane.shape, F32)
    for i in range(3):
        part = column.astype(BF16).astype(F32)
        terms = jnp.where(lane == i, part, terms)
        column = column - part
    return terms.astype(BF16)


def from_terms(tile):
    return jnp.sum(tile.astype(F32), axis=1, keepdims=True)


def products(k, xs, weights, outs):
    width = weights[0].shape[2] // lax.axis_size("col")
    for i, ref in enumerate(weights):
        x = xs[0][...] if len(xs) == 1 else jnp.concatenate([x[...] for x in xs], axis=0)
        both = dot(x, ref[0, :, block(k, width)])
        row = 0
        for out in outs:
            here = slice(row, row + out.shape[0])
            out[:, i * width : (i + 1) * width] = both[here].astype(out.dtype)
            row += out.shape[0]


def first(k, a_ref, b_ref, gain_ref, gate, up, x_out, s_out, out):
    rows = a_ref.shape[0]
    for i, ref in enumerate((a_ref, b_ref)):
        wide = ref[...].astype(F32)
        here = slice(i * rows, (i + 1) * rows)
        x_out[here, :] = (wide * gain_ref[...]).astype(BF16)
        s_out[here, :] = in_terms(jnp.sum(wide * wide, axis=1, keepdims=True))
    out[:, out.shape[1] - LANES :] = s_out[...]
    products(k, [x_out], (gate, up), (out,))


def two_products(ks, x, gate, up, a_out, b_out):
    products(ks[0], [x], (gate, up), (a_out,))
    products(ks[1], [x], (gate, up), (b_out,))


def product_of_both(k, xa, xb, gate, up, a_out, b_out):
    products(k, [xa, xb], (gate, up), (a_out, b_out))


def pause(value_ref, out):
    out[...] = value_ref[...]


def joined(p_ref, s_ref, r_ref, out):
    width = p_ref.shape[1]
    out[:, :width] = (p_ref[...].astype(F32) + r_ref[:, :width].astype(F32)).astype(BF16)
    out[:, width:] = in_terms(from_terms(s_ref[...]) + from_terms(r_ref[:, width:]))


def activate(factor, p_ref, near_ref, s_ref, far_ref, sib_ref, h_out):
    width = h_out.shape[1]
    tail = slice(2 * width, 2 * width + LANES)
    tiles = (s_ref[...], sib_ref[:, tail], far_ref[:, tail])
    inverse = lax.rsqrt(sum(from_terms(tile) for tile in tiles) * factor + EPS)
    gate, up = (
        (p_ref[:, at] + near_ref[:, at].astype(F32) + far_ref[:, at].astype(F32)) * inverse
        for at in (slice(0, width), slice(width, 2 * width))
    )
    h_out[...] = (gate / (1.0 + jnp.exp(-gate)) * up).astype(BF16)


def down(blocks, h, weight, out):
    for i, k in enumerate(blocks):
        out[i] = dot(h[...], weight[0, :, block(k, out.shape[2])]).astype(BF16)


def activate_and_down(factor, blocks, p, near, s, far, sib, weight, h_out, out):
    activate(factor, p, near, s, far, sib, h_out)
    down(blocks, h_out, weight, out)


def added(*values):
    return sum(v.astype(F32) for v in values).astype(BF16)


def sum_of_two(a_ref, b_ref, out):
    out[...] = added(a_ref[...], b_ref[...])


def fast(tokens, norm_gain, gate_weight, up_weight, down_weight):
    rows, cols, pipes = (lax.axis_size(a) for a in ("row", "col", "pipe"))
    _, count, depth = tokens.shape
    width = gate_weight.shape[2] // cols
    part = functools.partial
    own = tokens[0]
    m = rows // 2 * count
    forward = [(p, (p + 1) % pipes) for p in range(pipes)]
    slots = [own] + [swapped(own, "row", k) for k in range(1, rows)]
    payload, sums, wide = (((m, 2 * width + LANES), BF16), ((m, 2 * width), BF16), ((m, 2 * width), F32))
    x_shape, s_shape = ((m, depth), BF16), ((m, LANES), BF16)
    h_shape, e_shape = ((m, width), BF16), ((2, m, depth), BF16)
    weights = [gate_weight, up_weight]
    (gain,) = call(pause, "pause", [(norm_gain.shape, F32)], [norm_gain])

    xn, sn, p3n = call(
        part(first, 3), "first_near", [x_shape, s_shape, payload], [*slots[:2], gain, *weights]
    )
    r3n = swapped(p3n, "col", 1)
    p2n, p1n = call(part(two_products, (2, 1)), "next_near", [sums, sums], [xn, *weights])
    r1n = swapped(p1n, "col", 1)
    (q2n,) = call(joined, "joined_near", [payload], [p2n, sn, r3n])
    f2n = swapped(q2n, "col", 2)

    xf, sf, p3f = call(
        part(first, 3), "first_far", [x_shape, s_shape, payload], [*slots[2:], gain, *weights], (), [q2n]
    )
    r3f = swapped(p3f, "col", 1)
    p2f, p1f = call(
        part(two_products, (2, 1)), "next_far", [sums, sums], [xf, *weights], (), [p3f]
    )
    r1f = swapped(p1f, "col", 1)
    (q2f,) = call(joined, "joined_far", [payload], [p2f, sf, r3f])
    f2f = swapped(q2f, "col", 2)

    p0n, p0f = call(
        part(product_of_both, 0), "product0", [wide, wide], [xn, xf, *weights], (), [q2f]
    )

    def hidden_and_down(which, p0, r1, s, f2, r3, after):
        h, e1 = call(
            part(activate_and_down, 1.0 / (depth * cols), (1, 3)), "activate_" + which,
            [h_shape, e_shape], [p0, r1, s, f2, r3, down_weight], (), after,
        )
        t1 = swapped(e1, "col", 1)
        (e0,) = call(part(down, (0, 2)), "down_" + which, [e_shape], [h, down_weight], (), [e1])
        return e0, t1

    u = added(*hidden_and_down("near", p0n, r1n, sn, f2n, r3n, ()))
    n = added(u[0], swapped(u[1], "col", 2))
    e0f, t1f = hidden_and_down("far", p0f, r1f, sf, f2f, r3f, [u])
    (w,) = call(sum_of_two, "sum_far", [e_shape], [e0f, t1f], (), [])

    def onward(value, k):
        pairs = [(p * rows + r, q * rows + (r ^ k)) for p, q in forward for r in range(rows)]
        return lax.ppermute(value, ("pipe", "row"), pairs)

    own_part = onward(added(own, n[:count]), 0)
    near_part = onward(n[count:], 1)
    w = added(w[:, :count], swapped(w[:, count:], "row", 1))
    (w,) = call(sum_of_two, "sum_over_x", [(own.shape, BF16)], [w[0], swapped(w[1], "col", 2)], (), [own_part])
    return added(own_part, near_part, onward(w, 2))[None]


def plain(tokens, norm_gain, gate_weight, up_weight, down_weight):
    rows, cols, pipes = lax.axis_size("row"), lax.axis_size("col"), lax.axis_size("pipe")
    _, count, depth = tokens.shape
    wide = tokens[0].astype(F32)
    squares = lax.psum(jnp.sum(wide * wide, axis=1), "col")
    inverse = lax.rsqrt(squares / (depth * cols) + EPS)
    normed = (wide * inverse[:, None] * norm_gain).astype(BF16)
    piece = lax.all_gather(normed, "row", axis=0, tiled=True)
    sums = jnp.stack([dot(piece, gate_weight[0]), dot(piece, up_weight[0])])
    summed = lax.psum_scatter(sums.astype(BF16), "col", scatter_dimension=2, tiled=True).astype(F32)
    hidden = (jax.nn.silu(summed[0]) * summed[1]).astype(BF16)
    terms = dot(hidden, down_weight[0]).reshape(rows, count, cols, depth).transpose(0, 2, 1, 3)
    terms = terms.reshape(rows * cols, count, depth).astype(BF16)
    branch_out = lax.psum_scatter(terms, ("row", "col"), scatter_dimension=0, tiled=True)[0]
    layer_out = added(tokens[0], branch_out)
    return lax.ppermute(layer_out, "pipe", [(p, (p + 1) % pipes) for p in range(pipes)])[None]


def local(tokens, norm_gain, gate_weight, up_weight, down_weight):
    rows, cols = lax.axis_size("row"), lax.axis_size("col")
    _, count, depth = tokens.shape
    width = gate_weight.shape[2] // cols
    fits = (
        cols == 4
        and rows == 4
        and count % 16 == 0
        and depth % LANES == 0
        and width % LANES == 0
    )
    form = fast if fits else plain
    return form(tokens, norm_gain, gate_weight, up_weight, down_weight)


def solution(mesh):
    placed = (
        P("pipe", "row", "col"),
        P("pipe", "col"),
        P("pipe", "col", "row"),
        P("pipe", "col", "row"),
        P("pipe", ("row", "col"), None),
    )
    return jax.shard_map(
        local, mesh=mesh, in_specs=placed, out_specs=P("pipe", "row", "col"), check_vma=False
    )
```

```python
import functools

import jax
import jax.numpy as jnp
from jax import lax
from jax.experimental import pallas as pl
from jax.experimental.pallas import tpu as pltpu
from jax.sharding import PartitionSpec as P

EPS = 1e-05
LANES = 128
F32 = jnp.float32
BF16 = jnp.bfloat16


def flipped(index, mask):
    bit = 1
    while bit <= mask:
        if mask & bit:
            index = index + bit - 2 * bit * ((index // bit) % 2)
        bit *= 2
    return index


def swapped(value, axis, mask):
    count = lax.axis_size(axis)
    return lax.ppermute(value, axis, [(i, i ^ mask) for i in range(count)])


def masks_of(count):
    return [1 << b for b in range(count.bit_length() - 1)]


placed_in = pltpu.with_memory_space_constraint

COST = dict(
    pause=1000, first_near=100, next_near=100, first_far=100, next_far=100, joined_near=100, joined_far=100, product1=15, product0=1, activate_near=100, down_near=100, activate_far=100, down_far=1
)


def call(body, name, outs, held, streamed=(), after=(), copies=0):
    fixed = len(held) + len(streamed)

    def run(*refs):
        body(*refs[:fixed], *refs[fixed + len(after) :])

    spaces = [pltpu.VMEM] * len(held) + [pltpu.HBM] * len(streamed)
    return pl.pallas_call(
        run,
        name=name,
        in_specs=[pl.BlockSpec(memory_space=s) for s in spaces]
        + [pl.BlockSpec(memory_space=pl.ANY)] * len(after),
        out_shape=[pltpu.VMEM(shape, dtype) for shape, dtype in outs],
        out_specs=[pl.BlockSpec(memory_space=pltpu.VMEM)] * len(outs),
        scratch_shapes=[pltpu.SemaphoreType.DMA((copies,))] if copies else [],
        cost_estimate=pl.CostEstimate(
            flops=COST.get(name, 0) * 10**8, transcendentals=0, bytes_accessed=0
        ),
        compiler_params=pltpu.CompilerParams(vmem_limit_bytes=16 * 1024 * 1024),
    )(*[placed_in(a, s) for a, s in zip([*held, *streamed], spaces)], *after)


def dot(a, b):
    return jnp.dot(a, b, preferred_element_type=F32)


def block(k, width):
    return pl.ds(pl.multiple_of(flipped(lax.axis_index("col"), k) * width, LANES), width)


def in_terms(column):
    lane = lax.broadcasted_iota(jnp.int32, (column.shape[0], LANES), 1)
    terms = jnp.zeros(lane.shape, F32)
    for i in range(3):
        part = column.astype(BF16).astype(F32)
        terms = jnp.where(lane == i, part, terms)
        column = column - part
    return terms.astype(BF16)


def from_terms(tile):
    return jnp.sum(tile.astype(F32), axis=1, keepdims=True)


def products(k, xs, weights, outs):
    width = weights[0].shape[2] // lax.axis_size("col")
    for i, ref in enumerate(weights):
        x = xs[0][...] if len(xs) == 1 else jnp.concatenate([x[...] for x in xs], axis=0)
        both = dot(x, ref[0, :, block(k, width)])
        row = 0
        for out in outs:
            here = slice(row, row + out.shape[0])
            out[:, i * width : (i + 1) * width] = both[here].astype(out.dtype)
            row += out.shape[0]


def first(k, a_ref, b_ref, gain_ref, gate, up, x_out, s_out, out):
    rows = a_ref.shape[0]
    for i, ref in enumerate((a_ref, b_ref)):
        wide = ref[...].astype(F32)
        here = slice(i * rows, (i + 1) * rows)
        x_out[here, :] = (wide * gain_ref[...]).astype(BF16)
        s_out[here, :] = in_terms(jnp.sum(wide * wide, axis=1, keepdims=True))
    out[:, out.shape[1] - LANES :] = s_out[...]
    products(k, [x_out], (gate, up), (out,))


def two_products(ks, x, gate, up, a_out, b_out):
    products(ks[0], [x], (gate, up), (a_out,))
    products(ks[1], [x], (gate, up), (b_out,))


def product_of_both(k, xa, xb, gate, up, a_out, b_out):
    products(k, [xa, xb], (gate, up), (a_out, b_out))


def pause(value_ref, out):
    out[...] = value_ref[...]


def joined(p_ref, s_ref, r_ref, out):
    width = p_ref.shape[1]
    out[:, :width] = (p_ref[...].astype(F32) + r_ref[:, :width].astype(F32)).astype(BF16)
    out[:, width:] = in_terms(from_terms(s_ref[...]) + from_terms(r_ref[:, width:]))


def activate(factor, p_ref, near_ref, s_ref, far_ref, sib_ref, h_out):
    width = h_out.shape[1]
    tail = slice(2 * width, 2 * width + LANES)
    tiles = (s_ref[...], sib_ref[:, tail], far_ref[:, tail])
    inverse = lax.rsqrt(sum(from_terms(tile) for tile in tiles) * factor + EPS)
    gate, up = (
        (p_ref[:, at] + near_ref[:, at].astype(F32) + far_ref[:, at].astype(F32)) * inverse
        for at in (slice(0, width), slice(width, 2 * width))
    )
    h_out[...] = (gate / (1.0 + jnp.exp(-gate)) * up).astype(BF16)


def down(blocks, h, weight, out):
    for i, k in enumerate(blocks):
        out[i] = dot(h[...], weight[0, :, block(k, out.shape[2])]).astype(BF16)


def activate_and_down(factor, blocks, p, near, s, far, sib, weight, h_out, out):
    activate(factor, p, near, s, far, sib, h_out)
    down(blocks, h_out, weight, out)


def added(*values):
    return sum(v.astype(F32) for v in values).astype(BF16)


def sum_of_two(a_ref, b_ref, out):
    out[...] = added(a_ref[...], b_ref[...])


def sum_over_rows(both_ref, other_ref, out):
    out[...] = added(both_ref[:, : out.shape[1]], other_ref[...])


def near_sums(u_ref, other_ref, own_ref, a_out, b_out):
    count = a_out.shape[0]
    a_out[...] = added(own_ref[...], u_ref[0, :count], other_ref[:count])
    b_out[...] = added(u_ref[0, count:], other_ref[count:])


def fast(tokens, norm_gain, gate_weight, up_weight, down_weight):
    rows, cols, pipes = (lax.axis_size(a) for a in ("row", "col", "pipe"))
    _, count, depth = tokens.shape
    width = gate_weight.shape[2] // cols
    part = functools.partial
    own = tokens[0]
    m = rows // 2 * count
    forward = [(p, (p + 1) % pipes) for p in range(pipes)]
    slots = [own] + [swapped(own, "row", k) for k in range(1, rows)]
    payload, sums, wide = (((m, 2 * width + LANES), BF16), ((m, 2 * width), BF16), ((m, 2 * width), F32))
    x_shape, s_shape = ((m, depth), BF16), ((m, LANES), BF16)
    h_shape, e_shape = ((m, width), BF16), ((2, m, depth), BF16)
    weights = [gate_weight, up_weight]
    (gain,) = call(pause, "pause", [(norm_gain.shape, F32)], [norm_gain])

    xn, sn, p3n = call(
        part(first, 3), "first_near", [x_shape, s_shape, payload], [*slots[:2], gain, *weights]
    )
    r3n = swapped(p3n, "col", 1)
    p2n, p1n = call(part(two_products, (2, 1)), "next_near", [sums, sums], [xn, *weights])
    r1n = swapped(p1n, "col", 1)
    (q2n,) = call(joined, "joined_near", [payload], [p2n, sn, r3n])
    f2n = swapped(q2n, "col", 2)

    xf, sf, p3f = call(
        part(first, 3), "first_far", [x_shape, s_shape, payload], [*slots[2:], gain, *weights], (), [q2n]
    )
    r3f = swapped(p3f, "col", 1)
    p2f, p1f = call(
        part(two_products, (2, 1)), "next_far", [sums, sums], [xf, *weights], (), [p3f]
    )
    r1f = swapped(p1f, "col", 1)
    (q2f,) = call(joined, "joined_far", [payload], [p2f, sf, r3f])
    f2f = swapped(q2f, "col", 2)

    p0n, p0f = call(
        part(product_of_both, 0), "product0", [wide, wide], [xn, xf, *weights], (), [q2f]
    )

    def hidden_and_down(which, p0, r1, s, f2, r3, after):
        h, e1 = call(
            part(activate_and_down, 1.0 / (depth * cols), (1, 3)), "activate_" + which,
            [h_shape, e_shape], [p0, r1, s, f2, r3, down_weight], (), after,
        )
        t1 = swapped(e1, "col", 1)
        (e0,) = call(part(down, (0, 2)), "down_" + which, [e_shape], [h, down_weight], (), [e1])
        return e0, t1

    u = added(*hidden_and_down("near", p0n, r1n, sn, f2n, r3n, ()))
    un = swapped(u[1], "col", 2)
    e0f, t1f = hidden_and_down("far", p0f, r1f, sf, f2f, r3f, [u])
    (w,) = call(sum_of_two, "sum_far", [e_shape], [e0f, t1f], (), [])
    n0, n1 = call(near_sums, "sum_near", [(own.shape, BF16)] * 2, [u, un, own], (), [w])

    def onward(value, k):
        pairs = [(p * rows + r, q * rows + (r ^ k)) for p, q in forward for r in range(rows)]
        return lax.ppermute(value, ("pipe", "row"), pairs)

    own_part = onward(n0, 0)
    near_part = onward(n1, 1)
    (w,) = call(
        sum_over_rows, "sum_over_rows", [((2, *own.shape), BF16)],
        [w, swapped(w[:, count:], "row", 1)], (), [],
    )
    (w,) = call(sum_of_two, "sum_over_x", [(own.shape, BF16)], [w[0], swapped(w[1], "col", 2)], (), [])
    return added(own_part, near_part, onward(w, 2))[None]


def plain(tokens, norm_gain, gate_weight, up_weight, down_weight):
    rows, cols, pipes = lax.axis_size("row"), lax.axis_size("col"), lax.axis_size("pipe")
    _, count, depth = tokens.shape
    wide = tokens[0].astype(F32)
    squares = lax.psum(jnp.sum(wide * wide, axis=1), "col")
    inverse = lax.rsqrt(squares / (depth * cols) + EPS)
    normed = (wide * inverse[:, None] * norm_gain).astype(BF16)
    piece = lax.all_gather(normed, "row", axis=0, tiled=True)
    sums = jnp.stack([dot(piece, gate_weight[0]), dot(piece, up_weight[0])])
    summed = lax.psum_scatter(sums.astype(BF16), "col", scatter_dimension=2, tiled=True).astype(F32)
    hidden = (jax.nn.silu(summed[0]) * summed[1]).astype(BF16)
    terms = dot(hidden, down_weight[0]).reshape(rows, count, cols, depth).transpose(0, 2, 1, 3)
    terms = terms.reshape(rows * cols, count, depth).astype(BF16)
    branch_out = lax.psum_scatter(terms, ("row", "col"), scatter_dimension=0, tiled=True)[0]
    layer_out = added(tokens[0], branch_out)
    return lax.ppermute(layer_out, "pipe", [(p, (p + 1) % pipes) for p in range(pipes)])[None]


def local(tokens, norm_gain, gate_weight, up_weight, down_weight):
    rows, cols = lax.axis_size("row"), lax.axis_size("col")
    _, count, depth = tokens.shape
    width = gate_weight.shape[2] // cols
    fits = (
        cols == 4
        and rows == 4
        and count % 16 == 0
        and depth % LANES == 0
        and width % LANES == 0
    )
    form = fast if fits else plain
    return form(tokens, norm_gain, gate_weight, up_weight, down_weight)


def solution(mesh):
    placed = (
        P("pipe", "row", "col"),
        P("pipe", "col"),
        P("pipe", "col", "row"),
        P("pipe", "col", "row"),
        P("pipe", ("row", "col"), None),
    )
    return jax.shard_map(
        local, mesh=mesh, in_specs=placed, out_specs=P("pipe", "row", "col"), check_vma=False
    )
```

```python
import functools

import jax
import jax.numpy as jnp
from jax import lax
from jax.experimental import pallas as pl
from jax.experimental.pallas import tpu as pltpu
from jax.sharding import PartitionSpec as P

EPS = 1e-05
LANES = 128
F32 = jnp.float32
BF16 = jnp.bfloat16


def flipped(index, mask):
    bit = 1
    while bit <= mask:
        if mask & bit:
            index = index + bit - 2 * bit * ((index // bit) % 2)
        bit *= 2
    return index


def swapped(value, axis, mask):
    count = lax.axis_size(axis)
    return lax.ppermute(value, axis, [(i, i ^ mask) for i in range(count)])


def masks_of(count):
    return [1 << b for b in range(count.bit_length() - 1)]


placed_in = pltpu.with_memory_space_constraint

COST = dict(
    pause=1000, first_near=100, next_near=100, first_far=100, next_far=100, joined_near=100, joined_far=100, product1=15, product0=1, activate_near=100, down_near=100, activate_far=100, down_far=1
)


def call(body, name, outs, held, after=(), passed=()):
    own, last = len(held), len(held) + len(passed) + len(after)

    def run(*refs):
        body(*refs[:own], *refs[last : last + count])

    outs = [*outs, *((a.shape, a.dtype) for a in passed)]
    count = len(outs) - len(passed)
    vmem = pl.BlockSpec(memory_space=pltpu.VMEM)
    return pl.pallas_call(
        run,
        name=name,
        in_specs=[vmem] * (own + len(passed)) + [pl.BlockSpec(memory_space=pl.ANY)] * len(after),
        out_shape=[pltpu.VMEM(shape, dtype) for shape, dtype in outs],
        out_specs=[vmem] * len(outs),
        input_output_aliases={own + i: count + i for i in range(len(passed))},
        cost_estimate=pl.CostEstimate(
            flops=COST.get(name, 0) * 10**8, transcendentals=0, bytes_accessed=0
        ),
        compiler_params=pltpu.CompilerParams(vmem_limit_bytes=16 * 1024 * 1024),
    )(*[placed_in(a, pltpu.VMEM) for a in [*held, *passed]], *after)


def dot(a, b):
    return jnp.dot(a, b, preferred_element_type=F32)


def block(k, width):
    return pl.ds(pl.multiple_of(flipped(lax.axis_index("col"), k) * width, LANES), width)


def in_terms(column):
    lane = lax.broadcasted_iota(jnp.int32, (column.shape[0], LANES), 1)
    terms = jnp.zeros(lane.shape, F32)
    for i in range(3):
        part = column.astype(BF16).astype(F32)
        terms = jnp.where(lane == i, part, terms)
        column = column - part
    return terms.astype(BF16)


def from_terms(tile):
    return jnp.sum(tile.astype(F32), axis=1, keepdims=True)


def products(k, xs, weights, outs):
    width = weights[0].shape[2] // lax.axis_size("col")
    for i, ref in enumerate(weights):
        x = xs[0][...] if len(xs) == 1 else jnp.concatenate([x[...] for x in xs], axis=0)
        both = dot(x, ref[0, :, block(k, width)])
        row = 0
        for out in outs:
            here = slice(row, row + out.shape[0])
            out[:, i * width : (i + 1) * width] = both[here].astype(out.dtype)
            row += out.shape[0]


def first(k, a_ref, b_ref, gain_ref, gate, up, x_out, s_out, out):
    rows = a_ref.shape[0]
    for i, ref in enumerate((a_ref, b_ref)):
        wide = ref[...].astype(F32)
        here = slice(i * rows, (i + 1) * rows)
        x_out[here, :] = (wide * gain_ref[...]).astype(BF16)
        s_out[here, :] = in_terms(jnp.sum(wide * wide, axis=1, keepdims=True))
    out[:, out.shape[1] - LANES :] = s_out[...]
    products(k, [x_out], (gate, up), (out,))


def one_product(k, x, gate, up, out):
    products(k, [x], (gate, up), (out,))


def two_products(ks, x, gate, up, a_out, b_out):
    products(ks[0], [x], (gate, up), (a_out,))
    products(ks[1], [x], (gate, up), (b_out,))


def last_products(xn, xf, gate, up, a_out, b_out, c_out):
    products(0, [xn, xf], (gate, up), (a_out, b_out))
    products(1, [xf], (gate, up), (c_out,))


def pause(value_ref, out):
    out[...] = value_ref[...]


def joined(p_ref, s_ref, r_ref, out):
    width = p_ref.shape[1]
    out[:, :width] = (p_ref[...].astype(F32) + r_ref[:, :width].astype(F32)).astype(BF16)
    out[:, width:] = in_terms(from_terms(s_ref[...]) + from_terms(r_ref[:, width:]))


def activate(factor, p_ref, near_ref, s_ref, far_ref, sib_ref, h_out):
    width = h_out.shape[1]
    tail = slice(2 * width, 2 * width + LANES)
    tiles = (s_ref[...], sib_ref[:, tail], far_ref[:, tail])
    inverse = lax.rsqrt(sum(from_terms(tile) for tile in tiles) * factor + EPS)
    gate, up = (
        (p_ref[:, at] + near_ref[:, at].astype(F32) + far_ref[:, at].astype(F32)) * inverse
        for at in (slice(0, width), slice(width, 2 * width))
    )
    h_out[...] = (gate / (1.0 + jnp.exp(-gate)) * up).astype(BF16)


def down(blocks, h, weight, out):
    for i, k in enumerate(blocks):
        out[i] = dot(h[...], weight[0, :, block(k, out.shape[2])]).astype(BF16)


def activate_and_down(factor, blocks, p, near, s, far, sib, weight, h_out, out):
    activate(factor, p, near, s, far, sib, h_out)
    down(blocks, h_out, weight, out)


def added(*values):
    return sum(v.astype(F32) for v in values).astype(BF16)


def sum_of_two(a_ref, b_ref, out):
    out[...] = added(a_ref[...], b_ref[...])


def sum_over_rows(both_ref, other_ref, out):
    out[...] = added(both_ref[:, : out.shape[1]], other_ref[...])


def near_sums(u_ref, other_ref, own_ref, a_out, b_out):
    count = a_out.shape[0]
    a_out[...] = added(own_ref[...], u_ref[0, :count], other_ref[:count])
    b_out[...] = added(u_ref[0, count:], other_ref[count:])


def fast(tokens, norm_gain, gate_weight, up_weight, down_weight):
    rows, cols, pipes = (lax.axis_size(a) for a in ("row", "col", "pipe"))
    _, count, depth = tokens.shape
    width = gate_weight.shape[2] // cols
    part = functools.partial
    own = tokens[0]
    m = rows // 2 * count
    forward = [(p, (p + 1) % pipes) for p in range(pipes)]
    slots = [own] + [swapped(own, "row", k) for k in range(1, rows)]
    payload, sums, wide = (((m, 2 * width + LANES), BF16), ((m, 2 * width), BF16), ((m, 2 * width), F32))
    x_shape, s_shape = ((m, depth), BF16), ((m, LANES), BF16)
    h_shape, e_shape = ((m, width), BF16), ((2, m, depth), BF16)
    weights = [gate_weight, up_weight]
    (gain,) = call(pause, "pause", [(norm_gain.shape, F32)], [norm_gain], [slots[1]])

    xn, sn, p3n = call(
        part(first, 3), "first_near", [x_shape, s_shape, payload], [*slots[:2], gain, *weights]
    )
    r3n = swapped(p3n, "col", 1)
    p2n, p1n = call(part(two_products, (2, 1)), "next_near", [sums, sums], [xn, *weights])
    r1n = swapped(p1n, "col", 1)
    (q2n,) = call(joined, "joined_near", [payload], [p2n, sn, r3n])
    f2n = swapped(q2n, "col", 2)

    xf, sf, p3f = call(
        part(first, 3), "first_far", [x_shape, s_shape, payload], [*slots[2:], gain, *weights], [q2n]
    )
    r3f = swapped(p3f, "col", 1)
    (p2f,) = call(part(one_product, 2), "next_far", [sums], [xf, *weights], [p3f])
    (q2f,) = call(joined, "joined_far", [payload], [p2f, sf, r3f])
    f2f = swapped(q2f, "col", 2)

    p0n, p0f, p1f = call(
        last_products, "product0", [wide, wide, sums], [xn, xf, *weights], [q2f]
    )

    def hidden_and_down(which, p0, r1, s, f2, r3, after, passed=()):
        h, e1, *passed = call(
            part(activate_and_down, 1.0 / (depth * cols), (1, 3)), "activate_" + which,
            [h_shape, e_shape], [p0, r1, s, f2, r3, down_weight], after, passed,
        )
        t1 = swapped(e1, "col", 1)
        (e0,) = call(part(down, (0, 2)), "down_" + which, [e_shape], [h, down_weight], [e1])
        return e0, t1, *passed

    e0n, t1n, p1f = hidden_and_down("near", p0n, r1n, sn, f2n, r3n, (), [p1f])
    r1f = swapped(p1f, "col", 1)
    u = added(e0n, t1n)
    un = swapped(u[1], "col", 2)
    e0f, t1f = hidden_and_down("far", p0f, r1f, sf, f2f, r3f, [u])
    (w,) = call(sum_of_two, "sum_far", [e_shape], [e0f, t1f], [])
    n0, n1 = call(near_sums, "sum_near", [(own.shape, BF16)] * 2, [u, un, own], [w])

    def onward(value, k):
        pairs = [(p * rows + r, q * rows + (r ^ k)) for p, q in forward for r in range(rows)]
        return lax.ppermute(value, ("pipe", "row"), pairs)

    own_part = onward(n0, 0)
    near_part = onward(n1, 1)
    (w,) = call(
        sum_over_rows, "sum_over_rows", [((2, *own.shape), BF16)],
        [w, swapped(w[:, count:], "row", 1)], [],
    )
    (w,) = call(sum_of_two, "sum_over_x", [(own.shape, BF16)], [w[0], swapped(w[1], "col", 2)], [])
    return added(own_part, near_part, onward(w, 2))[None]


def plain(tokens, norm_gain, gate_weight, up_weight, down_weight):
    rows, cols, pipes = lax.axis_size("row"), lax.axis_size("col"), lax.axis_size("pipe")
    _, count, depth = tokens.shape
    wide = tokens[0].astype(F32)
    squares = lax.psum(jnp.sum(wide * wide, axis=1), "col")
    inverse = lax.rsqrt(squares / (depth * cols) + EPS)
    normed = (wide * inverse[:, None] * norm_gain).astype(BF16)
    piece = lax.all_gather(normed, "row", axis=0, tiled=True)
    sums = jnp.stack([dot(piece, gate_weight[0]), dot(piece, up_weight[0])])
    summed = lax.psum_scatter(sums.astype(BF16), "col", scatter_dimension=2, tiled=True).astype(F32)
    hidden = (jax.nn.silu(summed[0]) * summed[1]).astype(BF16)
    terms = dot(hidden, down_weight[0]).reshape(rows, count, cols, depth).transpose(0, 2, 1, 3)
    terms = terms.reshape(rows * cols, count, depth).astype(BF16)
    branch_out = lax.psum_scatter(terms, ("row", "col"), scatter_dimension=0, tiled=True)[0]
    layer_out = added(tokens[0], branch_out)
    return lax.ppermute(layer_out, "pipe", [(p, (p + 1) % pipes) for p in range(pipes)])[None]


def local(tokens, norm_gain, gate_weight, up_weight, down_weight):
    rows, cols = lax.axis_size("row"), lax.axis_size("col")
    _, count, depth = tokens.shape
    width = gate_weight.shape[2] // cols
    fits = (
        cols == 4
        and rows == 4
        and count % 16 == 0
        and depth % LANES == 0
        and width % LANES == 0
    )
    form = fast if fits else plain
    return form(tokens, norm_gain, gate_weight, up_weight, down_weight)


def solution(mesh):
    placed = (
        P("pipe", "row", "col"),
        P("pipe", "col"),
        P("pipe", "col", "row"),
        P("pipe", "col", "row"),
        P("pipe", ("row", "col"), None),
    )
    return jax.shard_map(
        local, mesh=mesh, in_specs=placed, out_specs=P("pipe", "row", "col"), check_vma=False
    )
```
